32 devices in a mesh: groups: 2 (over x), tensor: 16 (over z, y, core).
Axes of the slice: x: 2, y: 2, z: 4, core: 2. Of those that a mesh axis runs over, the one named last changes fastest.
Arguments:
- tokens: bfloat16 [4096, 4096], P(('groups', 'tensor')), parts along dimension 0, may hold values from -6 to 6
- cotangent: bfloat16 [4096, 4096], P(('groups', 'tensor')), parts along dimension 0, may hold values from -6 to 6
- w_in: bfloat16 [64, 2, 128, 128], P('tensor'), may hold values from -0.375 to 0.375
- w_out: bfloat16 [64, 2, 128, 128], P('tensor'), may hold values from -0.25 to 0.25
- index_in: int32 [64, 2], replicated, may hold values from 0 to 31, all different within a row
- index_out: int32 [64, 2], replicated, may hold values from 0 to 31, all different within a row
Outputs:
- output: bfloat16 [4096, 4096], P(('groups', 'tensor')), parts along dimension 0
- grad_tokens: bfloat16 [4096, 4096], P(('groups', 'tensor')), parts along dimension 0
- grad_in: float32 [128, 2, 128, 128], P(('groups', 'tensor')), parts along dimension 0
- grad_out: float32 [128, 2, 128, 128], P(('groups', 'tensor')), parts along dimension 0
The draws below stay inside these ranges and needn't reach their ends.
There are 2 independent parts, one for each index of `groups`. The reference program is written for one: setup_inputs(seed, part) draws one part's arguments, and reference() takes and returns one part's arrays. A program takes and returns all parts, laid end to end along the dimension named above; an argument that names none is the same for every part. Nothing has to cross between parts.
Inputs may be any that keep to these rules, and one draw needn't show every extreme that they name: Each row of index_in names 2 different block rows. Each row of index_out names 2 different block columns.
All inputs are finite; a program needn't handle non-finite values.
Results may differ from the reference program's by a relative error of at most 0.008.
Values may be sent and summed in bfloat16 or wider, within the bound.
No kernel may reach another device: no remote copies, remote signals or barrier semaphores. Data moves between devices by JAX's collectives and lax.ppermute only.
A program may use at most 128 MiB of HBM per device.

```python
import jax
import jax.numpy as jnp
from jax import lax

D = 4096
FF = 8192
BLOCK = 128
K = 2
TOK_DEV = 128
DB = 32
FFB = 64
TOKENS = 2048


def level_of(own_key, dims, shards, least, high):
    loudness = 1.0
    for position, shards_of in shards:
        steps = jax.random.uniform(jax.random.fold_in(jax.random.fold_in(own_key, 6), position), (shards_of,), jnp.float32, least / len(shards), high / len(shards))
        loudness = loudness * jnp.repeat(jnp.exp(steps), dims[position] // shards_of).reshape((-1,) + (1,) * (len(dims) - 1 - position))
    return loudness


def picks_of(key, rows, number_of, top, lift):
    order = jax.random.permutation(jax.random.fold_in(key, 1), number_of)
    favour = order
    for power in range(3):
        favour = favour * favour // number_of
    favour = favour * lift // number_of
    tickets = jax.random.randint(jax.random.fold_in(key, 2), (rows, number_of), 0, 4096) + favour
    holders = jax.random.permutation(jax.random.fold_in(key, 3), rows)[jnp.arange(number_of) % rows]
    tickets = jnp.where(jnp.arange(rows)[:, None] == holders[None, :], 1 << 14, tickets)
    priority = tickets * number_of + jnp.arange(number_of)
    return lax.top_k(priority.astype(jnp.int32), top)[1].astype(jnp.int32)


def centred(own_key, extent, scale, most, split=(), kind=jnp.bfloat16):
    drawn = scale * jax.random.normal(own_key, extent, jnp.float32)
    if split:
        drawn = drawn * level_of(own_key, extent, split, -0.22, 0.18)
    return jnp.clip(drawn, -most, most).astype(kind)


def setup_inputs(seed: int = 0, part: int = 0) -> dict:
    streams_of = jax.random.split(jax.random.key(seed), 7)
    own_keys = jax.random.split(jax.random.fold_in(streams_of[6], part), 7)
    return {
        "tokens": centred(own_keys[0], (TOKENS, D), 1.0, 6.0, ((0, 16),)),
        "cotangent": centred(own_keys[1], (TOKENS, D), 1.0, 6.0, ((0, 16),)),
        "w_in": centred(streams_of[2], (FFB, K, BLOCK, BLOCK), (K * BLOCK) ** -0.5, 0.375, ((0, 16),)),
        "w_out": centred(streams_of[3], (FFB, K, BLOCK, BLOCK), (FF * K // DB) ** -0.5, 0.25, ((0, 16),)),
        "index_in": picks_of(streams_of[4], FFB, DB, K, 0),
        "index_out": picks_of(streams_of[5], FFB, DB, K, 0),
    }


GELU_C = 0.7978845608
HIGH = lax.Precision.HIGHEST


def gelu_tanh(v):
    return 0.5 * v * (1.0 + jnp.tanh(GELU_C * (v + 0.044715 * v * v * v)))


def gelu_slope(v):
    s = jnp.tanh(GELU_C * (v + 0.044715 * v * v * v))
    return 0.5 * (1.0 + s) + 0.5 * v * (1.0 - s * s) * GELU_C * (1.0 + 3.0 * 0.044715 * v * v)


def reference(tokens, cotangent, w_in, w_out, index_in, index_out):
    rows = TOK_DEV
    count = TOKENS // rows
    onehot_in = (index_in[:, :, None] == jnp.arange(DB, dtype=jnp.int32)[None, None, :]).astype(jnp.float32)
    onehot_out = (index_out[:, :, None] == jnp.arange(DB, dtype=jnp.int32)[None, None, :]).astype(jnp.float32)
    weight_in = w_in.astype(jnp.float32)
    weight_out = w_out.astype(jnp.float32)

    def one_block(carry, pair):
        token_rows, cot_rows = pair
        picked = token_rows.reshape(rows, DB, BLOCK)[:, index_in].astype(jnp.float32)
        hidden_pre = jnp.einsum('tjki,jkio->tjo', picked, weight_in, precision=HIGH)
        act = gelu_tanh(hidden_pre).astype(jnp.bfloat16).astype(jnp.float32)
        partial_out = jnp.einsum('tjo,jkod->tjkd', act, weight_out, precision=HIGH)
        output = jnp.einsum('tjkd,jkb->tbd', partial_out, onehot_out, precision=HIGH)
        output = output.reshape(rows, D).astype(jnp.bfloat16)
        cot_picked = cot_rows.reshape(rows, DB, BLOCK)[:, index_out].astype(jnp.float32)
        grad_act = jnp.einsum('tjkd,jkod->tjo', cot_picked, weight_out, precision=HIGH)
        grad_pre = (grad_act * gelu_slope(hidden_pre)).astype(jnp.bfloat16).astype(jnp.float32)
        partial_back = jnp.einsum('tjo,jkio->tjki', grad_pre, weight_in, precision=HIGH)
        grad_rows = jnp.einsum('tjki,jkb->tbi', partial_back, onehot_in, precision=HIGH)
        grad_rows = grad_rows.reshape(rows, D).astype(jnp.bfloat16)
        sum_in = carry[0] + jnp.einsum('tjki,tjo->jkio', picked, grad_pre, precision=HIGH)
        sum_out = carry[1] + jnp.einsum('tjo,tjkd->jkod', act, cot_picked, precision=HIGH)
        return (sum_in, sum_out), (output, grad_rows)

    zeros = jnp.zeros((FFB, K, BLOCK, BLOCK), jnp.float32)
    pairs = (tokens.reshape(count, rows, D), cotangent.reshape(count, rows, D))
    (grad_in, grad_out), (output, grad_tokens) = lax.scan(one_block, (zeros, zeros), pairs)
    return output.reshape(TOKENS, D), grad_tokens.reshape(TOKENS, D), grad_in, grad_out
```

```python
import functools

import jax
import jax.numpy as jnp
from jax import lax
from jax.experimental import pallas as pl
from jax.experimental.pallas import tpu as pltpu
from jax.sharding import PartitionSpec as P

GELU_C = 0.7978845608
F32 = jnp.float32
BF16 = jnp.bfloat16


def dot(a, b, dims):
    return lax.dot_general(a, b, (dims, ((), ())), preferred_element_type=F32)


def ffn_kernel(lines, per, side, pos, idx_in, idx_out, *refs):
    pieces = 2 * lines - 1
    x_hbm, xo_hbm, c_hbm, co_hbm = refs[:4]
    weights = refs[4:4 + 4 * pieces]
    (out_own, gt_own, out_oth, gt_oth, gin0, gin1, gout0, gout1) = refs[4 + 4 * pieces:12 + 4 * pieces]
    (x, ct, win, wout, out_acc, gt_acc, tok_sem, w_sem) = refs[12 + 4 * pieces:]
    z, y, c = pos[0], pos[1], pos[2]
    rows = x_hbm.shape[0]

    loads = [
        pltpu.make_async_copy(x_hbm, x.at[pl.ds(0, rows)], tok_sem.at[0]),
        pltpu.make_async_copy(xo_hbm, x.at[pl.ds(rows, rows)], tok_sem.at[1]),
        pltpu.make_async_copy(c_hbm, ct.at[pl.ds(0, rows)], tok_sem.at[2]),
        pltpu.make_async_copy(co_hbm, ct.at[pl.ds(rows, rows)], tok_sem.at[3]),
    ]
    for load in loads:
        load.start()

    def fetch(piece, slot):
        for r in range(2):
            pltpu.make_async_copy(weights[4 * piece + 2 * r], win.at[slot, r], w_sem.at[slot]).start()
            pltpu.make_async_copy(weights[4 * piece + 2 * r + 1], wout.at[slot, r], w_sem.at[slot]).start()

    fetch(0, z)
    for s in range(1, lines):
        @pl.when(z >= s)
        def _():
            fetch(s, z - s)

        @pl.when(z + s < lines)
        def _():
            fetch(lines - 1 + s, z + s)

    out_acc[...] = jnp.zeros_like(out_acc)
    gt_acc[...] = jnp.zeros_like(gt_acc)
    for load in loads:
        load.wait()

    @pl.loop(0, lines)
    def _(slot):
        for r in range(2):
            pltpu.make_async_copy(weights[0], win.at[slot, r], w_sem.at[slot]).wait()
            pltpu.make_async_copy(weights[1], wout.at[slot, r], w_sem.at[slot]).wait()
        for r in range(2):
            gin, gout = ((gin0, gout0), (gin1, gout1))[r]
            core = c if r == 0 else 1 - c
            for m in range(per):
                j = ((slot * 2 + y) * 2 + core) * per + m
                a = [pl.ds(pl.multiple_of(idx_in[j, k] * side, side), side) for k in range(2)]
                b = [pl.ds(pl.multiple_of(idx_out[j, k] * side, side), side) for k in range(2)]
                p = jnp.concatenate([x[:, a[0]], x[:, a[1]]], axis=1)
                g = jnp.concatenate([ct[:, b[0]], ct[:, b[1]]], axis=1)
                wi = jnp.concatenate([win[slot, r, m, 0], win[slot, r, m, 1]], axis=0)
                wo = jnp.concatenate([wout[slot, r, m, 0], wout[slot, r, m, 1]], axis=1)
                h = dot(p, wi, ((1,), (0,)))
                ga = dot(g, wo, ((1,), (1,)))
                s = jnp.tanh(GELU_C * (h + 0.044715 * h * h * h))
                act = (0.5 * h * (1.0 + s)).astype(BF16)
                slope = 0.5 * (1.0 + s) + 0.5 * h * (1.0 - s * s) * GELU_C * (1.0 + 3.0 * 0.044715 * h * h)
                gp = (ga * slope).astype(BF16)
                po = dot(act, wo, ((1,), (0,)))
                pb = dot(gp, wi, ((1,), (1,)))
                gi = dot(p, gp, ((0,), (0,)))
                go = dot(act, g, ((0,), (0,)))
                for k in range(2):
                    out_acc[:, b[k]] += po[:, k * side:(k + 1) * side]
                    gt_acc[:, a[k]] += pb[:, k * side:(k + 1) * side]
                    gin[slot, m, k] = gi[k * side:(k + 1) * side].astype(gin.dtype)
                    gout[slot, m, k] = go[:, k * side:(k + 1) * side].astype(gout.dtype)

    out_own[...] = out_acc[:rows]
    gt_own[...] = gt_acc[:rows]
    out_oth[...] = out_acc[rows:].astype(BF16)
    gt_oth[...] = gt_acc[rows:].astype(BF16)


def local(size, tokens, cotangent, w_in, w_out, index_in, index_out):
    rows, width = tokens.shape
    per, _, side, _ = w_in.shape
    lines = size // 4
    me = lax.axis_index("tensor")
    z, y, c = me // 4, (me // 2) % 2, me % 2
    core_swap = [(i, i ^ 1) for i in range(size)]
    y_swap = [(i, i ^ 2) for i in range(size)]

    def pp(v, perm):
        return lax.ppermute(v, "tensor", perm)

    tokens_oth = pp(tokens, y_swap)
    cot_oth = pp(cotangent, y_swap)
    up_hop = [(i, i + 4) for i in range(size - 4)]
    down_hop = [(i + 4, i) for i in range(size - 4)]
    own = (w_in, w_out)
    from_below, from_above = [], []
    low, high = own, own
    for s in range(1, lines):
        low = tuple(pp(v, up_hop) for v in low)
        high = tuple(pp(v, down_hop) for v in high)
        from_below.append(low)
        from_above.append(high)
    pieces = [own] + from_below + from_above
    operands = []
    for n, piece in enumerate(pieces):
        if n == 0:
            who = range(size)
        elif n < lines:
            who = [i for i in range(size) if i // 4 >= n]
        else:
            who = [i for i in range(size) if i // 4 + (n - lines + 1) < lines]
        swap = [(i, i ^ 1) for i in who]
        operands += list(piece) + [pp(v, swap) for v in piece]

    pos = jnp.stack([z, y, c]).astype(jnp.int32)
    smem = pl.BlockSpec(memory_space=pltpu.SMEM)
    hbm = pl.BlockSpec(memory_space=pl.ANY)
    vmem = pl.BlockSpec(memory_space=pltpu.VMEM)
    shape = jax.ShapeDtypeStruct
    wide = (lines, per, 2, side, side)
    out_own, gt_own, out_oth, gt_oth, gin0, gin1, gout0, gout1 = pl.pallas_call(
        functools.partial(ffn_kernel, lines, per, side),
        out_shape=(
            shape((rows, width), F32), shape((rows, width), F32),
            shape((rows, width), BF16), shape((rows, width), BF16),
            shape(wide, F32), shape(wide, BF16), shape(wide, F32), shape(wide, BF16),
        ),
        in_specs=[smem] * 3 + [hbm] * (4 + len(operands)),
        out_specs=(vmem,) * 8,
        scratch_shapes=[
            pltpu.VMEM((2 * rows, width), BF16),
            pltpu.VMEM((2 * rows, width), BF16),
            pltpu.VMEM((lines, 2, per, 2, side, side), BF16),
            pltpu.VMEM((lines, 2, per, 2, side, side), BF16),
            pltpu.VMEM((2 * rows, width), F32),
            pltpu.VMEM((2 * rows, width), F32),
            pltpu.SemaphoreType.DMA((4,)),
            pltpu.SemaphoreType.DMA((lines,)),
        ],
        compiler_params=pltpu.CompilerParams(vmem_limit_bytes=52 * 1024 * 1024),
    )(pos, index_in, index_out, tokens, tokens_oth, cotangent, cot_oth, *operands)

    out_back = pp(out_oth, y_swap)
    gt_back = pp(gt_oth, y_swap)

    def reduce_line(mine, partner):
        def at(i):
            return (lax.dynamic_index_in_dim(mine, i, 0, keepdims=False)
                    + lax.dynamic_index_in_dim(partner, i, 0, keepdims=False).astype(F32))

        up = down = None
        for step in range(1, lines):
            far = lines - step
            send_up, send_down = at(z + far), at(z - far)
            if step > 1:
                send_up = send_up + up.astype(F32)
                send_down = send_down + down.astype(F32)
            up = pp(send_up.astype(BF16), [(i, i + 4) for i in range(size - 4) if i // 4 < step])
            down = pp(send_down.astype(BF16), [(i, i - 4) for i in range(4, size) if i // 4 >= lines - step])
        total = at(z)
        if lines > 1:
            total = total + up.astype(F32) + down.astype(F32)
        return total

    grad_in = reduce_line(gin0, pp(gin1, core_swap))
    grad_out = reduce_line(gout0, pp(gout1, core_swap))
    output = (out_own + out_back.astype(F32)).astype(BF16)
    grad_tokens = (gt_own + gt_back.astype(F32)).astype(BF16)
    return output, grad_tokens, grad_in, grad_out


def solution(mesh):
    size = mesh.shape["tensor"]
    in_specs = (
        P(("groups", "tensor"), None),
        P(("groups", "tensor"), None),
        P("tensor", None, None, None),
        P("tensor", None, None, None),
        P(),
        P(),
    )
    out_specs = (
        P(("groups", "tensor"), None),
        P(("groups", "tensor"), None),
        P(("groups", "tensor"), None, None, None),
        P(("groups", "tensor"), None, None, None),
    )
    return jax.shard_map(functools.partial(local, size), mesh=mesh, in_specs=in_specs, out_specs=out_specs, check_vma=False)
```

```python
import functools

import jax
import jax.numpy as jnp
from jax import lax
from jax.experimental import pallas as pl
from jax.experimental.pallas import tpu as pltpu
from jax.sharding import PartitionSpec as P

GELU_C = 0.7978845608
F32 = jnp.float32
BF16 = jnp.bfloat16


def dot(a, b, dims):
    return lax.dot_general(a, b, (dims, ((), ())), preferred_element_type=F32)


def column_of(pos, lines, per, r, m):
    owner = lax.rem(pos[0] - r + lines, lines)
    return ((owner * 2 + pos[1]) * 2 + pos[2]) * per + m


def blocks_of(index, column, side):
    return [pl.ds(pl.multiple_of(index[column, k] * side, side), side) for k in range(2)]


def start_rows(parts, buf, sem):
    loads, first = [], 0
    for n, part in enumerate(parts):
        rows = part.shape[0]
        loads.append(pltpu.make_async_copy(part, buf.at[pl.ds(first, rows)], sem.at[n]))
        loads[-1].start()
        first += rows
    return loads


def store_quarters(acc, quarters, rounded, rows, sem):
    stores = []
    for n in (3, 1, 2, 0):
        part = pl.ds(n * rows, rows)
        rounded[part] = acc[part].astype(BF16)
        stores.append(pltpu.make_async_copy(rounded.at[part], quarters[n], sem.at[n]))
        stores[-1].start()
    return stores


def ffn_kernel(lines, per, side, pos, idx_in, idx_out, *refs):
    xs, cs, refs = refs[:4], refs[4:8], refs[8:]
    pieces, refs = refs[:1 + lines], refs[1 + lines:]
    outs, gts, refs = refs[:4], refs[4:8], refs[8:]
    g_own, g_send, refs = refs[0], refs[1:lines], refs[lines:]
    x, ct, w, out_acc, gt_acc, g_v, s_v, x_sem, c_sem, w_sem, o_sem, g_sem = refs
    rows = outs[0].shape[0]
    loads = start_rows(xs, x, x_sem)
    loads += start_rows(cs, ct, c_sem)
    for r in range(1, lines):
        pltpu.make_async_copy(pieces[1 + r], w.at[r], w_sem.at[r]).start()
    pltpu.make_async_copy(pieces[0], w.at[0, 0], w_sem.at[0]).start()
    pltpu.make_async_copy(pieces[1], w.at[0, 1], w_sem.at[0]).start()
    out_acc[...] = jnp.zeros_like(out_acc)
    gt_acc[...] = jnp.zeros_like(gt_acc)
    for load in loads:
        load.wait()

    def line(r, put):
        pltpu.make_async_copy(pieces[0], w.at[r, 0], w_sem.at[r]).wait()
        pltpu.make_async_copy(pieces[1], w.at[r, 1], w_sem.at[r]).wait()
        for m in range(per):
            j = column_of(pos, lines, per, r, m)
            a, b = blocks_of(idx_in, j, side), blocks_of(idx_out, j, side)
            p = jnp.concatenate([x[:, a[0]], x[:, a[1]]], axis=1)
            g = jnp.concatenate([ct[:, b[0]], ct[:, b[1]]], axis=1)
            wi = jnp.concatenate([w[r, 0, m, 0], w[r, 0, m, 1]], axis=0)
            wo = jnp.concatenate([w[r, 1, m, 0], w[r, 1, m, 1]], axis=1)
            h = dot(p, wi, ((1,), (0,)))
            ga = dot(g, wo, ((1,), (1,)))
            h2 = h * h
            s = jnp.tanh(h * (GELU_C + GELU_C * 0.044715 * h2))
            act = (0.5 * h * (1.0 + s)).astype(BF16)
            slope = 0.5 * (1.0 + s) + (0.5 * h) * (1.0 - s * s) * (GELU_C + GELU_C * 3.0 * 0.044715 * h2)
            gp = (ga * slope).astype(BF16)
            po = dot(act, wo, ((1,), (0,)))
            pb = dot(gp, wi, ((1,), (1,)))
            gi = dot(p, gp, ((0,), (0,)))
            go = dot(act, g, ((0,), (0,)))
            for k in range(2):
                out_acc[:, b[k]] += po[:, k * side:(k + 1) * side]
                gt_acc[:, a[k]] += pb[:, k * side:(k + 1) * side]
                put(m, k, gi[k * side:(k + 1) * side], go[:, k * side:(k + 1) * side])

    @pl.loop(1, lines)
    def _(r):
        def put(m, k, gi, go):
            s_v[r - 1, 0, m, k] = gi.astype(BF16)
            s_v[r - 1, 1, m, k] = go.astype(BF16)
        line(r, put)

    stores = [pltpu.make_async_copy(s_v.at[r - 1], g_send[r - 1], g_sem.at[r]) for r in range(1, lines)]
    for store in stores:
        store.start()

    def put(m, k, gi, go):
        g_v[0, m, k] = gi
        g_v[1, m, k] = go
    line(0, put)
    stores.append(pltpu.make_async_copy(g_v, g_own, g_sem.at[0]))
    stores[-1].start()
    stores += store_quarters(out_acc, outs, x, rows, o_sem.at[0])
    stores += store_quarters(gt_acc, gts, ct, rows, o_sem.at[1])
    for store in stores:
        store.wait()


def local(size, tokens, cotangent, w_in, w_out, index_in, index_out):
    rows, width = tokens.shape
    per, _, side, _ = w_in.shape
    lines = size // 4
    me = lax.axis_index("tensor")
    z, y, c = me // 4, (me // 2) % 2, me % 2
    core_swap = [(i, i ^ 1) for i in range(size)]
    y_swap = [(i, i ^ 2) for i in range(size)]

    def pp(v, perm):
        return lax.ppermute(v, "tensor", perm)

    def turn(r):
        return [(i, (i + 4 * r) % size) for i in range(size)]

    def after(v, *done):
        return lax.optimization_barrier((v, *done))[0]

    x_far = pp(tokens, y_swap)
    c_far = pp(cotangent, y_swap)
    both = jnp.stack([w_in, w_out])
    directs = [pp(both, turn(r)) for r in range(1, lines)]
    x_near = pp(after(tokens, *directs[-1:]), core_swap)
    c_near = pp(after(cotangent, *directs[-1:]), core_swap)
    x_diag = pp(after(x_far, *directs), core_swap)
    c_diag = pp(after(c_far, *directs), core_swap)
    operands = (tokens, x_near, x_far, x_diag, cotangent, c_near, c_far, c_diag, w_in, w_out, *directs)

    pos = jnp.stack([z, y, c]).astype(jnp.int32)
    smem = pl.BlockSpec(memory_space=pltpu.SMEM)
    hbm = pl.BlockSpec(memory_space=pl.ANY)
    shape = jax.ShapeDtypeStruct
    packed = (2, per, 2, side, side)
    token_buf = pltpu.VMEM((4 * rows, width), BF16)
    acc_buf = pltpu.VMEM((4 * rows, width), F32)
    dma = pltpu.SemaphoreType.DMA
    res = pl.pallas_call(
        functools.partial(ffn_kernel, lines, per, side),
        out_shape=(shape((rows, width), BF16),) * 8 + (shape(packed, F32),) + (shape(packed, BF16),) * (lines - 1),
        in_specs=[smem] * 3 + [hbm] * len(operands),
        out_specs=(hbm,) * (8 + lines),
        scratch_shapes=[token_buf, token_buf, pltpu.VMEM((lines,) + packed, BF16), acc_buf, acc_buf,
                        pltpu.VMEM(packed, F32), pltpu.VMEM((max(lines - 1, 1),) + packed, BF16),
                        dma((4,)), dma((4,)), dma((lines,)), dma((2, 4)), dma((lines,))],
        compiler_params=pltpu.CompilerParams(vmem_limit_bytes=31 * 1024 * 1024),
        cost_estimate=pl.CostEstimate(flops=24 * rows * lines * per * 2 * side * side * 2,
                                      bytes_accessed=24 << 20, transcendentals=0),
    )(pos, index_in, index_out, *operands)
    outs, gts, g_own, g_send = res[:4], res[4:8], res[8], res[9:]

    def far_sum(parts):
        return (parts[2].astype(F32) + pp(parts[3], core_swap).astype(F32)).astype(BF16)

    out_far, gt_far = far_sum(outs), far_sum(gts)
    out_near, gt_near = pp(outs[1], core_swap), pp(gts[1], core_swap)
    received = [pp(after(g_send[r - 1], out_far, gt_far, out_near, gt_near), turn(-r)) for r in range(1, lines)]
    out_back, gt_back = pp(out_far, y_swap), pp(gt_far, y_swap)
    output = (outs[0].astype(F32) + out_near.astype(F32) + out_back.astype(F32)).astype(BF16)
    total = g_own
    for recv in received:
        total = total + recv.astype(F32)
    grad_tokens = (gts[0].astype(F32) + gt_near.astype(F32) + gt_back.astype(F32)).astype(BF16)
    return output, grad_tokens, total[0], total[1]


def solution(mesh):
    in_specs = (
        P(("groups", "tensor"), None),
        P(("groups", "tensor"), None),
        P("tensor", None, None, None),
        P("tensor", None, None, None),
        P(),
        P(),
    )
    out_specs = (
        P(("groups", "tensor"), None),
        P(("groups", "tensor"), None),
        P(("groups", "tensor"), None, None, None),
        P(("groups", "tensor"), None, None, None),
    )
    fn = functools.partial(local, mesh.shape["tensor"])
    return jax.shard_map(fn, mesh=mesh, in_specs=in_specs, out_specs=out_specs, check_vma=False)
```

```python
import functools

import jax
import jax.numpy as jnp
from jax import lax
from jax.experimental import pallas as pl
from jax.experimental.pallas import tpu as pltpu
from jax.sharding import PartitionSpec as P

GELU_C = 0.7978845608
F32 = jnp.float32
BF16 = jnp.bfloat16


def dot(a, b, dims):
    return lax.dot_general(a, b, (dims, ((), ())), preferred_element_type=F32)


def blocks_of(scalars, lines, per, side, r, m):
    owner = lax.rem(scalars[0] - r + lines, lines)
    first = 3 + 2 * (((owner * 2 + scalars[1]) * 2 + scalars[2]) * per + m)
    count = 8 * lines * per

    def block(at):
        return pl.ds(pl.multiple_of(scalars[at] * side, side), side)

    return [block(first), block(first + 1)], [block(first + count), block(first + count + 1)]


def start_rows(parts, buf, sem):
    loads, first = [], 0
    for n, part in enumerate(parts):
        rows = part.shape[0]
        loads.append(pltpu.make_async_copy(part, buf.at[pl.ds(first, rows)], sem.at[n]))
        loads[-1].start()
        first += rows
    return loads


def store_quarters(acc, quarters, rounded, rows, sem):
    stores = []
    for n in (3, 1, 2, 0):
        part = pl.ds(n * rows, rows)
        rounded[part] = acc[part].astype(BF16)
        stores.append(pltpu.make_async_copy(rounded.at[part], quarters[n], sem.at[n]))
        stores[-1].start()
    return stores


def ffn_kernel(lines, per, side, scalars, *refs):
    xs, cs, refs = refs[:4], refs[4:8], refs[8:]
    pieces, sums, refs = refs[:lines], refs[lines:lines + 4], refs[lines + 4:]
    outs, gts = [part.at[0] for part in sums], [part.at[1] for part in sums]
    g_own, g_send, refs = refs[0], refs[1:lines], refs[lines:]
    x, ct, w, out_acc, gt_acc, g_v, s_v, x_sem, c_sem, w_sem, o_sem, g_sem = refs
    rows = outs[0].shape[0]
    loads = start_rows(xs, x, x_sem)
    loads += start_rows(cs, ct, c_sem)
    for r in [*range(1, lines), 0]:
        pltpu.make_async_copy(pieces[r], w.at[r], w_sem.at[r]).start()
    out_acc[...] = jnp.zeros_like(out_acc)
    gt_acc[...] = jnp.zeros_like(gt_acc)
    for load in loads:
        load.wait()

    def line(r, put):
        pltpu.make_async_copy(pieces[0], w.at[r], w_sem.at[r]).wait()
        for m in range(per):
            a, b = blocks_of(scalars, lines, per, side, r, m)
            p = jnp.concatenate([x[:, a[0]], x[:, a[1]]], axis=1)
            g = jnp.concatenate([ct[:, b[0]], ct[:, b[1]]], axis=1)
            wi = jnp.concatenate([w[r, 0, m, 0], w[r, 0, m, 1]], axis=0)
            wo = jnp.concatenate([w[r, 1, m, 0], w[r, 1, m, 1]], axis=1)
            h = dot(p, wi, ((1,), (0,)))
            ga = dot(g, wo, ((1,), (1,)))
            h2 = h * h
            s = jnp.tanh(h * (GELU_C + GELU_C * 0.044715 * h2))
            act = (0.5 * h * (1.0 + s)).astype(BF16)
            slope = 0.5 * (1.0 + s) + (0.5 * h) * (1.0 - s * s) * (GELU_C + GELU_C * 3.0 * 0.044715 * h2)
            gp = (ga * slope).astype(BF16)
            po = dot(act, wo, ((1,), (0,)))
            pb = dot(gp, wi, ((1,), (1,)))
            gi = dot(p, gp, ((0,), (0,)))
            go = dot(act, g, ((0,), (0,)))
            for k in range(2):
                out_acc[:, b[k]] += po[:, k * side:(k + 1) * side]
                gt_acc[:, a[k]] += pb[:, k * side:(k + 1) * side]
                put(m, k, gi[k * side:(k + 1) * side], go[:, k * side:(k + 1) * side])

    @pl.loop(1, lines)
    def _(r):
        def put(m, k, gi, go):
            s_v[r - 1, 0, m, k] = gi.astype(BF16)
            s_v[r - 1, 1, m, k] = go.astype(BF16)
        line(r, put)

    stores = [pltpu.make_async_copy(s_v.at[r - 1], g_send[r - 1], g_sem.at[r]) for r in range(1, lines)]
    for store in stores:
        store.start()

    def put(m, k, gi, go):
        g_v[0, m, k] = gi
        g_v[1, m, k] = go
    line(0, put)
    stores.append(pltpu.make_async_copy(g_v, g_own, g_sem.at[0]))
    stores[-1].start()
    stores += store_quarters(out_acc, outs, x, rows, o_sem.at[0])
    stores += store_quarters(gt_acc, gts, ct, rows, o_sem.at[1])
    for store in stores:
        store.wait()


def local(size, tokens, cotangent, w_in, w_out, index_in, index_out):
    rows, width = tokens.shape
    per, _, side, _ = w_in.shape
    lines = size // 4
    me = lax.axis_index("tensor")
    z, y, c = me // 4, (me // 2) % 2, me % 2
    core_swap = [(i, i ^ 1) for i in range(size)]
    y_swap = [(i, i ^ 2) for i in range(size)]

    def pp(v, perm):
        return lax.ppermute(v, "tensor", perm)

    def turn(r):
        return [(i, (i + 4 * r) % size) for i in range(size)]

    def after(v, *done):
        return lax.optimization_barrier((v, *done))[0]

    x_far = pp(tokens, y_swap)
    c_far = pp(cotangent, y_swap)
    both = jnp.stack([w_in, w_out])
    directs = [pp(both, turn(r)) for r in range(1, lines)]
    scalars = jnp.concatenate([jnp.stack([z, y, c]), index_in.reshape(-1), index_out.reshape(-1)]).astype(jnp.int32)
    x_own, scalars, _ = lax.optimization_barrier((tokens, scalars, directs[-1]))
    c_own, _ = lax.optimization_barrier((cotangent, directs[0]))
    x_near = pp(x_own, core_swap)
    c_near = pp(c_own, core_swap)
    x_diag = pp(after(x_far, *directs[:1]), core_swap)
    c_diag = pp(after(c_far, *directs), core_swap)
    operands = (x_own, x_near, x_far, x_diag, c_own, c_near, c_far, c_diag, both, *directs)

    smem = pl.BlockSpec(memory_space=pltpu.SMEM)
    hbm = pl.BlockSpec(memory_space=pltpu.HBM)
    shape = jax.ShapeDtypeStruct
    packed = (2, per, 2, side, side)
    token_buf = pltpu.VMEM((4 * rows, width), BF16)
    acc_buf = pltpu.VMEM((4 * rows, width), F32)
    dma = pltpu.SemaphoreType.DMA
    res = pl.pallas_call(
        functools.partial(ffn_kernel, lines, per, side),
        out_shape=(shape((2, rows, width), BF16),) * 4 + (shape(packed, F32),) + (shape(packed, BF16),) * (lines - 1),
        in_specs=[smem] + [hbm] * len(operands),
        out_specs=(hbm,) * (4 + lines),
        scratch_shapes=[token_buf, token_buf, pltpu.VMEM((lines,) + packed, BF16), acc_buf, acc_buf,
                        pltpu.VMEM(packed, F32), pltpu.VMEM((max(lines - 1, 1),) + packed, BF16),
                        dma((4,)), dma((4,)), dma((lines,)), dma((2, 4)), dma((lines,))],
        compiler_params=pltpu.CompilerParams(vmem_limit_bytes=31 * 1024 * 1024),
        cost_estimate=pl.CostEstimate(flops=24 * rows * lines * per * 2 * side * side * 2,
                                      bytes_accessed=24 << 20, transcendentals=0),
    )(scalars, *operands)
    own, near, far, diagonal, g_own, *g_send = res
    far = (far.astype(F32) + pp(diagonal, core_swap).astype(F32)).astype(BF16)
    received = [pp(after(g, far), turn(-r)) for r, g in enumerate(g_send, 1)]
    near = pp(after(near, far), core_swap)
    back = pp(far, y_swap)
    output, grad_tokens = [(own[n].astype(F32) + near[n].astype(F32) + back[n].astype(F32)).astype(BF16)
                           for n in range(2)]
    total = g_own
    for recv in received:
        total = total + recv.astype(F32)
    return output, grad_tokens, total[0], total[1]


def solution(mesh):
    in_specs = (
        P(("groups", "tensor"), None),
        P(("groups", "tensor"), None),
        P("tensor", None, None, None),
        P("tensor", None, None, None),
        P(),
        P(),
    )
    out_specs = (
        P(("groups", "tensor"), None),
        P(("groups", "tensor"), None),
        P(("groups", "tensor"), None, None, None),
        P(("groups", "tensor"), None, None, None),
    )
    fn = functools.partial(local, mesh.shape["tensor"])
    return jax.shard_map(fn, mesh=mesh, in_specs=in_specs, out_specs=out_specs, check_vma=False)
```

```python
import functools

import jax
import jax.numpy as jnp
from jax import lax
from jax.experimental import pallas as pl
from jax.experimental.pallas import tpu as pltpu
from jax.sharding import PartitionSpec as P

GELU_C = 0.7978845608
F32 = jnp.float32
BF16 = jnp.bfloat16


def dot(a, b, dims):
    return lax.dot_general(a, b, (dims, ((), ())), preferred_element_type=F32)


def blocks_of(scalars, lines, per, side, r, m):
    owner = lax.rem(scalars[0] - r + lines, lines)
    first = 4 + 2 * (((owner * 2 + scalars[1]) * 2 + scalars[2]) * per + m)
    count = 8 * lines * per

    def block(at):
        return pl.ds(pl.multiple_of(scalars[at] * side, side), side)

    return [block(first), block(first + 1)], [block(first + count), block(first + count + 1)]


def start_rows(parts, buf, sem):
    loads, first = [], 0
    for n, part in enumerate(parts):
        rows = part.shape[0]
        loads.append(pltpu.make_async_copy(part, buf.at[pl.ds(first, rows)], sem.at[n]))
        loads[-1].start()
        first += rows
    return loads


def store_halves(acc, halves, rounded, rows, sem):
    stores = []
    for n in (1, 0):
        part = pl.ds(n * rows, rows)
        rounded[part] = acc[part].astype(BF16)
        stores.append(pltpu.make_async_copy(rounded.at[part], halves[n], sem.at[n]))
        stores[-1].start()
    return stores


def fetch_weights(lines, half, pieces, halves, w, sem):
    for r in range(1, lines):
        if r == lines // 2:
            @pl.when(half == 0)
            def _():
                pltpu.make_async_copy(halves[0], w.at[r, 0], sem.at[r]).start()
                pltpu.make_async_copy(halves[1], w.at[r, 1], sem.at[r]).start()

            @pl.when(half != 0)
            def _():
                pltpu.make_async_copy(halves[1], w.at[r, 0], sem.at[r]).start()
                pltpu.make_async_copy(halves[0], w.at[r, 1], sem.at[r]).start()
        else:
            pltpu.make_async_copy(pieces[r], w.at[r], sem.at[r]).start()
    pltpu.make_async_copy(pieces[0], w.at[0], sem.at[0]).start()


def ffn_kernel(lines, per, side, last, scalars, *refs):
    parts = 4 if last else 2
    xs, cs, refs = refs[:2], refs[2:2 + parts], refs[2 + parts:]
    halves, refs = refs[:2], refs[2:]
    pieces, refs = list(refs[:lines - 1]), refs[lines - 1:]
    pieces.insert(lines // 2, None)
    if last:
        before, sums, g_own = refs[0], refs[1:3], refs[3]
        g_send, refs = refs[4:3 + lines], refs[3 + lines:]
    else:
        sums, g_all, refs = refs[:2], refs[2], refs[3:]
    outs, gts = [part.at[0] for part in sums], [part.at[1] for part in sums]
    x, ct, w, out_acc, gt_acc, g_v, s_v, x_sem, c_sem, w_sem, b_sem, o_sem, g_sem = refs
    rows = xs[0].shape[0]
    loads = start_rows(xs, x, x_sem) + start_rows(cs, ct, c_sem)
    fetch_weights(lines, scalars[3], pieces, halves, w, w_sem)
    if last:
        for r in range(lines):
            pltpu.make_async_copy(before.at[r], g_v.at[r], b_sem.at[r]).start()
    out_acc[...] = jnp.zeros_like(out_acc)
    gt_acc[...] = jnp.zeros_like(gt_acc)
    for load in loads:
        load.wait()

    def line(r, put):
        pltpu.make_async_copy(pieces[0], w.at[r], w_sem.at[r]).wait()
        if last:
            pltpu.make_async_copy(before.at[r], g_v.at[r], b_sem.at[r]).wait()
        for m in range(per):
            a, b = blocks_of(scalars, lines, per, side, r, m)
            p = jnp.concatenate([x[:, a[0]], x[:, a[1]]], axis=1)
            g = jnp.concatenate([ct[:, b[0]], ct[:, b[1]]], axis=1)
            wi = jnp.concatenate([w[r, 0, m, 0], w[r, 0, m, 1]], axis=0)
            wo = jnp.concatenate([w[r, 1, m, 0], w[r, 1, m, 1]], axis=1)
            h = dot(p, wi, ((1,), (0,)))
            ga = dot(g, wo, ((1,), (1,)))
            h2 = h * h
            s = jnp.tanh(h * (GELU_C + GELU_C * 0.044715 * h2))
            act = (0.5 * h * (1.0 + s)).astype(BF16)
            slope = 0.5 * (1.0 + s) + (0.5 * h) * (1.0 - s * s) * (GELU_C + GELU_C * 3.0 * 0.044715 * h2)
            gp = (ga * slope).astype(BF16)
            po = dot(act, wo, ((1,), (0,)))
            pb = dot(gp, wi, ((1,), (1,)))
            gi = dot(p, gp, ((0,), (0,)))
            go = dot(act, g, ((0,), (0,)))
            for k in range(2):
                out_acc[:, b[k]] += po[:, k * side:(k + 1) * side]
                gt_acc[:, a[k]] += pb[:, k * side:(k + 1) * side]
                put(m, k, gi[k * side:(k + 1) * side], go[:, k * side:(k + 1) * side])

    def keep(r):
        def put(m, k, gi, go):
            g_v[r, 0, m, k] = g_v[r, 0, m, k] + gi if last else gi
            g_v[r, 1, m, k] = g_v[r, 1, m, k] + go if last else go
        return put

    def send(r):
        def put(m, k, gi, go):
            s_v[r - 1, 0, m, k] = (g_v[r, 0, m, k] + gi).astype(BF16)
            s_v[r - 1, 1, m, k] = (g_v[r, 1, m, k] + go).astype(BF16)
        return put

    @pl.loop(1, lines)
    def _(r):
        line(r, send(r) if last else keep(r))

    if last:
        stores = [pltpu.make_async_copy(s_v.at[r - 1], g_send[r - 1], g_sem.at[r]) for r in range(1, lines)]
        for store in stores:
            store.start()
    line(0, keep(0))
    if last:
        stores.append(pltpu.make_async_copy(g_v.at[0], g_own, g_sem.at[0]))
    else:
        stores = [pltpu.make_async_copy(g_v, g_all, g_sem.at[0])]
    stores[-1].start()
    stores += store_halves(out_acc, outs, x, rows, o_sem.at[0])
    stores += store_halves(gt_acc, gts, ct, rows, o_sem.at[1])
    for store in stores:
        store.wait()


def local(size, groups, tokens, cotangent, w_in, w_out, index_in, index_out):
    rows, width = tokens.shape
    per, _, side, _ = w_in.shape
    lines = size // 4
    me = lax.axis_index("tensor")
    half = lax.axis_index("groups") % 2
    z, y, c = me // 4, (me // 2) % 2, me % 2
    core_swap = [(i, i ^ 1) for i in range(size)]
    y_swap = [(i, i ^ 2) for i in range(size)]
    group_swap = [(i, i ^ 1) for i in range(groups)]

    def pp(v, perm, axis="tensor"):
        return lax.ppermute(v, axis, perm)

    def turn(r):
        return [(i, (i + 4 * r) % size) for i in range(size)]

    def after(v, *done):
        return lax.optimization_barrier((v, *done))[0]

    x_far = pp(tokens, y_swap)
    upper = rows * 5 // 8
    c_upper = pp(cotangent[:upper], y_swap)
    c_lower = pp(after(cotangent[upper:], c_upper), y_swap)
    both = jnp.stack([w_in, w_out])
    middle = lines // 2
    sent = [both] * lines
    sent[middle] = jnp.where(half == 0, w_in, w_out)
    first = pp(sent[middle], turn(middle))
    directs = [both]
    for r in range(1, lines):
        if r == middle:
            directs.append(first)
        else:
            directs.append(pp(after(both, first) if r > middle else both, turn(r)))
    halves = [directs[middle], pp(directs[middle], group_swap, "groups")]
    place = jnp.stack([z, y, c, half])
    scalars = jnp.concatenate([place, index_in.reshape(-1), index_out.reshape(-1)]).astype(jnp.int32)
    x_own, scalars, _, _ = lax.optimization_barrier((tokens, scalars, directs[-1], halves[1]))
    c_own = after(cotangent, directs[1])
    x_near = pp(x_own, core_swap)
    c_near = pp(c_own, core_swap)
    x_diag = pp(after(x_far, c_upper), core_swap)
    x_near = after(x_near, x_diag)

    smem = pl.BlockSpec(memory_space=pltpu.SMEM)
    hbm = pl.BlockSpec(memory_space=pltpu.HBM)
    shape = jax.ShapeDtypeStruct
    packed = (2, per, 2, side, side)
    token_buf = pltpu.VMEM((2 * rows, width), BF16)
    acc_buf = pltpu.VMEM((2 * rows, width), F32)
    dma = pltpu.SemaphoreType.DMA

    def call(last, out_shape, *operands):
        return pl.pallas_call(
            functools.partial(ffn_kernel, lines, per, side, last),
            out_shape=(shape((2, rows, width), BF16),) * 2 + out_shape,
            in_specs=[smem] + [hbm] * len(operands),
            out_specs=(hbm,) * (2 + len(out_shape)),
            scratch_shapes=[token_buf, token_buf, pltpu.VMEM((lines,) + packed, BF16), acc_buf, acc_buf,
                            pltpu.VMEM((lines,) + packed, F32), pltpu.VMEM((max(lines - 1, 1),) + packed, BF16),
                            dma((2,)), dma((4,)), dma((lines,)), dma((lines,)), dma((2, 2)), dma((lines,))],
            compiler_params=pltpu.CompilerParams(vmem_limit_bytes=24 * 1024 * 1024),
            cost_estimate=pl.CostEstimate(flops=1 << 20, bytes_accessed=1 << 20, transcendentals=0),
        )(scalars, *operands)

    weights = (*halves, *directs[:middle], *directs[middle + 1:])
    own, near, g_all = call(False, (shape((lines,) + packed, F32),), x_own, x_near, c_own, c_near, *weights)
    c_lower = after(c_lower, own)
    c_far = (c_upper, c_lower)
    c_diag = [pp(part, core_swap) for part in c_far]
    far, diagonal, g_own, *g_send = call(
        True, (shape(packed, F32),) + (shape(packed, BF16),) * (lines - 1),
        x_far, x_diag, *c_far, *c_diag, *weights, g_all)

    far = (far.astype(F32) + pp(diagonal, core_swap).astype(F32)).astype(BF16)
    received = [pp(after(g, far), turn(-r)) for r, g in enumerate(g_send, 1)]
    near = pp(after(near, far), core_swap)
    back = pp(far, y_swap)
    output, grad_tokens = [(own[n].astype(F32) + near[n].astype(F32) + back[n].astype(F32)).astype(BF16)
                           for n in range(2)]
    total = g_own
    for recv in received:
        total = total + recv.astype(F32)
    return output, grad_tokens, total[0], total[1]


def solution(mesh):
    in_specs = (
        P(("groups", "tensor"), None),
        P(("groups", "tensor"), None),
        P("tensor", None, None, None),
        P("tensor", None, None, None),
        P(),
        P(),
    )
    out_specs = (
        P(("groups", "tensor"), None),
        P(("groups", "tensor"), None),
        P(("groups", "tensor"), None, None, None),
        P(("groups", "tensor"), None, None, None),
    )
    fn = functools.partial(local, mesh.shape["tensor"], mesh.shape["groups"])
    return jax.shard_map(fn, mesh=mesh, in_specs=in_specs, out_specs=out_specs, check_vma=False)
```

```python
import functools

import jax
import jax.numpy as jnp
from jax import lax
from jax.experimental import pallas as pl
from jax.experimental.pallas import tpu as pltpu
from jax.sharding import PartitionSpec as P

GELU_C = 0.7978845608
F32 = jnp.float32
BF16 = jnp.bfloat16


def dot(a, b, dims):
    return lax.dot_general(a, b, (dims, ((), ())), preferred_element_type=F32)


def blocks_of(scalars, lines, per, side, r, m):
    owner = lax.rem(scalars[0] - r + lines, lines)
    first = 4 + 2 * (((owner * 2 + scalars[1]) * 2 + scalars[2]) * per + m)
    count = 8 * lines * per

    def block(at):
        return pl.ds(pl.multiple_of(scalars[at] * side, side), side)

    return [block(first), block(first + 1)], [block(first + count), block(first + count + 1)]


def start_rows(parts, buf, sem):
    loads, first = [], 0
    for n, part in enumerate(parts):
        rows = part.shape[0]
        loads.append(pltpu.make_async_copy(part, buf.at[pl.ds(first, rows)], sem.at[n]))
        loads[-1].start()
        first += rows
    return loads


def store_halves(acc, halves, rounded, rows, sem):
    stores = []
    for n in (1, 0):
        part = pl.ds(n * rows, rows)
        rounded[part] = acc[part].astype(BF16)
        stores.append(pltpu.make_async_copy(rounded.at[part], halves[n], sem.at[n]))
        stores[-1].start()
    return stores


def fetch_weights(lines, half, pieces, halves, w, sem):
    for r in range(1, lines):
        if r == lines // 2:
            @pl.when(half == 0)
            def _():
                pltpu.make_async_copy(halves[0], w.at[r, 0], sem.at[r]).start()
                pltpu.make_async_copy(halves[1], w.at[r, 1], sem.at[r]).start()

            @pl.when(half != 0)
            def _():
                pltpu.make_async_copy(halves[1], w.at[r, 0], sem.at[r]).start()
                pltpu.make_async_copy(halves[0], w.at[r, 1], sem.at[r]).start()
        else:
            pltpu.make_async_copy(pieces[r], w.at[r], sem.at[r]).start()
    pltpu.make_async_copy(pieces[0], w.at[0], sem.at[0]).start()


def ffn_kernel(lines, per, side, last, scalars, *refs):
    parts = 4 if last else 2
    xs, cs, refs = refs[:2], refs[2:2 + parts], refs[2 + parts:]
    halves, refs = refs[:2], refs[2:]
    pieces, refs = list(refs[:lines - 1]), refs[lines - 1:]
    pieces.insert(lines // 2, None)
    if last:
        before, sums, g_own = refs[0], refs[1:3], refs[3]
        g_send, refs = refs[4:3 + lines], refs[3 + lines:]
    else:
        sums, g_all, refs = refs[:2], refs[2], refs[3:]
    outs, gts = [part.at[0] for part in sums], [part.at[1] for part in sums]
    x, ct, w, out_acc, gt_acc, g_v, s_v, x_sem, c_sem, w_sem, b_sem, o_sem, g_sem = refs
    rows = xs[0].shape[0]
    loads = start_rows(xs, x, x_sem) + start_rows(cs, ct, c_sem)
    fetch_weights(lines, scalars[3], pieces, halves, w, w_sem)
    if last:
        for r in range(lines):
            pltpu.make_async_copy(before.at[r], g_v.at[r], b_sem.at[r]).start()
    out_acc[...] = jnp.zeros_like(out_acc)
    gt_acc[...] = jnp.zeros_like(gt_acc)
    for load in loads:
        load.wait()

    def line(r, put):
        pltpu.make_async_copy(pieces[0], w.at[r], w_sem.at[r]).wait()
        if last:
            pltpu.make_async_copy(before.at[r], g_v.at[r], b_sem.at[r]).wait()
        for m in range(per):
            a, b = blocks_of(scalars, lines, per, side, r, m)
            p = jnp.concatenate([x[:, a[0]], x[:, a[1]]], axis=1)
            g = jnp.concatenate([ct[:, b[0]], ct[:, b[1]]], axis=1)
            wi = jnp.concatenate([w[r, 0, m, 0], w[r, 0, m, 1]], axis=0)
            wo = jnp.concatenate([w[r, 1, m, 0], w[r, 1, m, 1]], axis=1)
            h = dot(p, wi, ((1,), (0,)))
            ga = dot(g, wo, ((1,), (1,)))
            h2 = h * h
            s = jnp.tanh(h * (GELU_C + GELU_C * 0.044715 * h2))
            act = (0.5 * h * (1.0 + s)).astype(BF16)
            slope = 0.5 * (1.0 + s) + (0.5 * h) * (1.0 - s * s) * (GELU_C + GELU_C * 3.0 * 0.044715 * h2)
            gp = (ga * slope).astype(BF16)
            po = dot(act, wo, ((1,), (0,)))
            pb = dot(gp, wi, ((1,), (1,)))
            gi = dot(p, gp, ((0,), (0,)))
            go = dot(act, g, ((0,), (0,)))
            for k in range(2):
                out_acc[:, b[k]] += po[:, k * side:(k + 1) * side]
                gt_acc[:, a[k]] += pb[:, k * side:(k + 1) * side]
                put(m, k, gi[k * side:(k + 1) * side], go[:, k * side:(k + 1) * side])

    def keep(r):
        def put(m, k, gi, go):
            g_v[r, 0, m, k] = g_v[r, 0, m, k] + gi if last else gi
            g_v[r, 1, m, k] = g_v[r, 1, m, k] + go if last else go
        return put

    def send(r):
        def put(m, k, gi, go):
            s_v[r - 1, 0, m, k] = (g_v[r, 0, m, k] + gi).astype(BF16)
            s_v[r - 1, 1, m, k] = (g_v[r, 1, m, k] + go).astype(BF16)
        return put

    @pl.loop(1, lines)
    def _(r):
        line(r, send(r) if last else keep(r))

    if last:
        stores = [pltpu.make_async_copy(s_v.at[r - 1], g_send[r - 1], g_sem.at[r]) for r in range(1, lines)]
        for store in stores:
            store.start()
    line(0, keep(0))
    if last:
        stores.append(pltpu.make_async_copy(g_v.at[0], g_own, g_sem.at[0]))
    else:
        stores = [pltpu.make_async_copy(g_v, g_all, g_sem.at[0])]
    stores[-1].start()
    stores += store_halves(out_acc, outs, x, rows, o_sem.at[0])
    stores += store_halves(gt_acc, gts, ct, rows, o_sem.at[1])
    for store in stores:
        store.wait()


def local(size, groups, tokens, cotangent, w_in, w_out, index_in, index_out):
    rows, width = tokens.shape
    per, _, side, _ = w_in.shape
    lines = size // 4
    me = lax.axis_index("tensor")
    half = lax.axis_index("groups") % 2
    z, y, c = me // 4, (me // 2) % 2, me % 2
    core_swap = [(i, i ^ 1) for i in range(size)]
    y_swap = [(i, i ^ 2) for i in range(size)]
    group_swap = [(i, i ^ 1) for i in range(groups)]

    def pp(v, perm, axis="tensor"):
        return lax.ppermute(v, axis, perm)

    def turn(r):
        return [(i, (i + 4 * r) % size) for i in range(size)]

    def after(v, *done):
        return lax.optimization_barrier((v, *done))[0]

    x_far = pp(tokens, y_swap)
    upper = rows * 5 // 8
    c_upper = pp(cotangent[:upper], y_swap)
    c_lower = pp(after(cotangent[upper:], c_upper), y_swap)
    both = jnp.stack([w_in, w_out])
    middle = lines // 2
    sent = [both] * lines
    sent[middle] = jnp.where(half == 0, w_in, w_out)
    first = pp(sent[middle], turn(middle))
    directs = [both]
    for r in range(1, lines):
        if r == middle:
            directs.append(first)
        else:
            directs.append(pp(after(both, first) if r > middle else both, turn(r)))
    halves = [directs[middle], pp(directs[middle], group_swap, "groups")]
    place = jnp.stack([z, y, c, half])
    scalars = jnp.concatenate([place, index_in.reshape(-1), index_out.reshape(-1)]).astype(jnp.int32)
    x_own, scalars, _, _ = lax.optimization_barrier((tokens, scalars, directs[-1], halves[1]))
    c_own = after(cotangent, directs[1])
    x_near = pp(x_own, core_swap)
    c_near = pp(c_own, core_swap)
    x_diag = pp(after(x_far, c_upper), core_swap)
    x_near = after(x_near, x_diag)

    smem = pl.BlockSpec(memory_space=pltpu.SMEM)
    hbm = pl.BlockSpec(memory_space=pltpu.HBM)
    shape = jax.ShapeDtypeStruct
    packed = (2, per, 2, side, side)
    token_buf = pltpu.VMEM((2 * rows, width), BF16)
    acc_buf = pltpu.VMEM((2 * rows, width), F32)
    dma = pltpu.SemaphoreType.DMA

    def call(last, out_shape, *operands):
        return pl.pallas_call(
            functools.partial(ffn_kernel, lines, per, side, last),
            out_shape=(shape((2, rows, width), BF16),) * 2 + out_shape,
            in_specs=[smem] + [hbm] * len(operands),
            out_specs=(hbm,) * (2 + len(out_shape)),
            scratch_shapes=[token_buf, token_buf, pltpu.VMEM((lines,) + packed, BF16), acc_buf, acc_buf,
                            pltpu.VMEM((lines,) + packed, F32), pltpu.VMEM((max(lines - 1, 1),) + packed, BF16),
                            dma((2,)), dma((4,)), dma((lines,)), dma((lines,)), dma((2, 2)), dma((lines,))],
            compiler_params=pltpu.CompilerParams(vmem_limit_bytes=24 * 1024 * 1024),
            cost_estimate=pl.CostEstimate(flops=1 << 20, bytes_accessed=1 << 20, transcendentals=0),
        )(scalars, *operands)

    weights = (*halves, *directs[:middle], *directs[middle + 1:])
    own, near, g_all = call(False, (shape((lines,) + packed, F32),), x_own, x_near, c_own, c_near, *weights)
    c_lower = after(c_lower, own)
    c_far = (c_upper, c_lower)
    c_diag = [pp(part, core_swap) for part in c_far]
    far, diagonal, g_own, *g_send = call(
        True, (shape(packed, F32),) + (shape(packed, BF16),) * (lines - 1),
        x_far, x_diag, *c_far, *c_diag, *weights, g_all)

    far = (far.astype(F32) + pp(diagonal, core_swap).astype(F32)).astype(BF16)
    received = [pp(after(g, far), turn(-r)) for r, g in enumerate(g_send, 1)]
    near = pp(after(near, far), core_swap)
    back = pp(far, y_swap)
    output, grad_tokens = [(own[n].astype(F32) + near[n].astype(F32) + back[n].astype(F32)).astype(BF16)
                           for n in range(2)]
    grads = []
    for n in range(2):
        total = g_own[n]
        for recv in received:
            total = total + recv[n].astype(F32)
        grads.append(total)
    return output, grad_tokens, grads[0], grads[1]


def solution(mesh):
    in_specs = (
        P(("groups", "tensor"), None),
        P(("groups", "tensor"), None),
        P("tensor", None, None, None),
        P("tensor", None, None, None),
        P(),
        P(),
    )
    out_specs = (
        P(("groups", "tensor"), None),
        P(("groups", "tensor"), None),
        P(("groups", "tensor"), None, None, None),
        P(("groups", "tensor"), None, None, None),
    )
    fn = functools.partial(local, mesh.shape["tensor"], mesh.shape["groups"])
    return jax.shard_map(fn, mesh=mesh, in_specs=in_specs, out_specs=out_specs, check_vma=False)
```

```python
import functools

import jax
import jax.numpy as jnp
from jax import lax
from jax.experimental import pallas as pl
from jax.experimental.pallas import tpu as pltpu
from jax.sharding import PartitionSpec as P

GELU_C = 0.7978845608
F32 = jnp.float32
BF16 = jnp.bfloat16


def dot(a, b, dims):
    return lax.dot_general(a, b, (dims, ((), ())), preferred_element_type=F32)


def blocks_of(scalars, lines, per, side, r, m):
    owner = lax.rem(scalars[0] - r + lines, lines)
    first = 4 + 2 * (((owner * 2 + scalars[1]) * 2 + scalars[2]) * per + m)
    count = 8 * lines * per

    def block(at):
        return pl.ds(pl.multiple_of(scalars[at] * side, side), side)

    return [block(first), block(first + 1)], [block(first + count), block(first + count + 1)]


def start_rows(parts, buf, sem):
    loads, first = [], 0
    for n, part in enumerate(parts):
        rows = part.shape[0]
        loads.append(pltpu.make_async_copy(part, buf.at[pl.ds(first, rows)], sem.at[n]))
        loads[-1].start()
        first += rows
    return loads


def store_halves(acc, halves, rounded, rows, sem):
    stores = []
    for n in (1, 0):
        part = pl.ds(n * rows, rows)
        rounded[part] = acc[part].astype(BF16)
        stores.append(pltpu.make_async_copy(rounded.at[part], halves[n], sem.at[n]))
        stores[-1].start()
    return stores


def fetch_weights(lines, half, pieces, halves, w, sem):
    for r in range(1, lines):
        if r == lines // 2:
            @pl.when(half == 0)
            def _():
                pltpu.make_async_copy(halves[0], w.at[r, 0], sem.at[r]).start()
                pltpu.make_async_copy(halves[1], w.at[r, 1], sem.at[r]).start()

            @pl.when(half != 0)
            def _():
                pltpu.make_async_copy(halves[1], w.at[r, 0], sem.at[r]).start()
                pltpu.make_async_copy(halves[0], w.at[r, 1], sem.at[r]).start()
        else:
            pltpu.make_async_copy(pieces[r], w.at[r], sem.at[r]).start()
    pltpu.make_async_copy(pieces[0], w.at[0], sem.at[0]).start()


def ffn_kernel(lines, per, side, last, scalars, *refs):
    parts = 4 if last else 2
    xs, cs, refs = refs[:2], refs[2:2 + parts], refs[2 + parts:]
    halves, refs = refs[:2], refs[2:]
    pieces, refs = list(refs[:lines - 1]), refs[lines - 1:]
    pieces.insert(lines // 2, None)
    if last:
        before, sums, g_own = refs[0], refs[1:3], refs[3]
        g_send, refs = refs[4:3 + lines], refs[3 + lines:]
    else:
        sums, g_all, refs = refs[:2], refs[2], refs[3:]
    outs, gts = [part.at[0] for part in sums], [part.at[1] for part in sums]
    x, ct, w, out_acc, gt_acc, g_v, s_v, x_sem, c_sem, w_sem, b_sem, o_sem, g_sem = refs
    rows = xs[0].shape[0]
    loads = start_rows(xs, x, x_sem) + start_rows(cs, ct, c_sem)
    fetch_weights(lines, scalars[3], pieces, halves, w, w_sem)
    if last:
        for r in range(lines):
            pltpu.make_async_copy(before.at[r], g_v.at[r], b_sem.at[r]).start()
    out_acc[...] = jnp.zeros_like(out_acc)
    gt_acc[...] = jnp.zeros_like(gt_acc)
    for load in loads:
        load.wait()

    def line(r, put):
        pltpu.make_async_copy(pieces[0], w.at[r], w_sem.at[r]).wait()
        if last:
            pltpu.make_async_copy(before.at[r], g_v.at[r], b_sem.at[r]).wait()
        for m in range(per):
            a, b = blocks_of(scalars, lines, per, side, r, m)
            p = jnp.concatenate([x[:, a[0]], x[:, a[1]]], axis=1)
            g = jnp.concatenate([ct[:, b[0]], ct[:, b[1]]], axis=1)
            wi = jnp.concatenate([w[r, 0, m, 0], w[r, 0, m, 1]], axis=0)
            wo = jnp.concatenate([w[r, 1, m, 0], w[r, 1, m, 1]], axis=1)
            h = dot(p, wi, ((1,), (0,)))
            ga = dot(g, wo, ((1,), (1,)))
            h2 = h * h
            s = jnp.tanh(h * (GELU_C + GELU_C * 0.044715 * h2))
            act = (0.5 * h * (1.0 + s)).astype(BF16)
            slope = 0.5 * (1.0 + s) + (0.5 * h) * (1.0 - s * s) * (GELU_C + GELU_C * 3.0 * 0.044715 * h2)
            gp = (ga * slope).astype(BF16)
            po = dot(act, wo, ((1,), (0,)))
            pb = dot(gp, wi, ((1,), (1,)))
            gi = dot(p, gp, ((0,), (0,)))
            go = dot(act, g, ((0,), (0,)))
            for k in range(2):
                out_acc[:, b[k]] += po[:, k * side:(k + 1) * side]
                gt_acc[:, a[k]] += pb[:, k * side:(k + 1) * side]
                put(m, k, gi[k * side:(k + 1) * side], go[:, k * side:(k + 1) * side])

    def keep(r):
        def put(m, k, gi, go):
            g_v[r, 0, m, k] = g_v[r, 0, m, k] + gi if last else gi
            g_v[r, 1, m, k] = g_v[r, 1, m, k] + go if last else go
        return put

    def send(r):
        def put(m, k, gi, go):
            s_v[r - 1, 0, m, k] = (g_v[r, 0, m, k] + gi).astype(BF16)
            s_v[r - 1, 1, m, k] = (g_v[r, 1, m, k] + go).astype(BF16)
        return put

    @pl.loop(1, lines)
    def _(r):
        line(r, send(r) if last else keep(r))

    if last:
        stores = [pltpu.make_async_copy(s_v.at[r - 1], g_send[r - 1], g_sem.at[r]) for r in range(1, lines)]
        for store in stores:
            store.start()
    line(0, keep(0))
    if last:
        stores.append(pltpu.make_async_copy(g_v.at[0], g_own, g_sem.at[0]))
    else:
        stores = [pltpu.make_async_copy(g_v, g_all, g_sem.at[0])]
    stores[-1].start()
    stores += store_halves(out_acc, outs, x, rows, o_sem.at[0])
    stores += store_halves(gt_acc, gts, ct, rows, o_sem.at[1])
    for store in stores:
        store.wait()


def local(size, groups, tokens, cotangent, w_in, w_out, index_in, index_out):
    rows, width = tokens.shape
    per, _, side, _ = w_in.shape
    lines = size // 4
    me = lax.axis_index("tensor")
    half = lax.axis_index("groups") % 2
    z, y, c = me // 4, (me // 2) % 2, me % 2
    core_swap = [(i, i ^ 1) for i in range(size)]
    y_swap = [(i, i ^ 2) for i in range(size)]
    group_swap = [(i, i ^ 1) for i in range(groups)]

    def pp(v, perm, axis="tensor"):
        return lax.ppermute(v, axis, perm)

    def turn(r):
        return [(i, (i + 4 * r) % size) for i in range(size)]

    def after(v, *done):
        return lax.optimization_barrier((v, *done))[0]

    x_far = pp(tokens, y_swap)
    upper = rows * 5 // 8
    c_upper = pp(cotangent[:upper], y_swap)
    c_lower = pp(after(cotangent[upper:], c_upper), y_swap)
    both = jnp.stack([w_in, w_out])
    middle = lines // 2
    sent = [both] * lines
    sent[middle] = jnp.where(half == 0, w_in, w_out)
    first = pp(sent[middle], turn(middle))
    directs = [both]
    for r in range(1, lines):
        if r == middle:
            directs.append(first)
        else:
            directs.append(pp(after(both, first) if r > middle else both, turn(r)))
    halves = [directs[middle], pp(directs[middle], group_swap, "groups")]
    place = jnp.stack([z, y, c, half])
    scalars = jnp.concatenate([place, index_in.reshape(-1), index_out.reshape(-1)]).astype(jnp.int32)
    x_own, scalars, _, _ = lax.optimization_barrier((tokens, scalars, directs[-1], halves[1]))
    c_own = after(cotangent, directs[1])
    x_near = pp(x_own, core_swap)
    c_near = pp(c_own, core_swap)
    x_diag = pp(after(x_far, c_upper), core_swap)
    x_near = after(x_near, x_diag)

    smem = pl.BlockSpec(memory_space=pltpu.SMEM)
    hbm = pl.BlockSpec(memory_space=pltpu.HBM)
    shape = jax.ShapeDtypeStruct
    packed = (2, per, 2, side, side)
    token_buf = pltpu.VMEM((2 * rows, width), BF16)
    acc_buf = pltpu.VMEM((2 * rows, width), F32)
    dma = pltpu.SemaphoreType.DMA

    def call(last, out_shape, *operands):
        return pl.pallas_call(
            functools.partial(ffn_kernel, lines, per, side, last),
            out_shape=(shape((2, rows, width), BF16),) * 2 + out_shape,
            in_specs=[smem] + [hbm] * len(operands),
            out_specs=(hbm,) * (2 + len(out_shape)),
            scratch_shapes=[token_buf, token_buf, pltpu.VMEM((lines,) + packed, BF16), acc_buf, acc_buf,
                            pltpu.VMEM((lines,) + packed, F32), pltpu.VMEM((max(lines - 1, 1),) + packed, BF16),
                            dma((2,)), dma((4,)), dma((lines,)), dma((lines,)), dma((2, 2)), dma((lines,))],
            compiler_params=pltpu.CompilerParams(vmem_limit_bytes=24 * 1024 * 1024),
            cost_estimate=pl.CostEstimate(flops=1 << 20, bytes_accessed=1 << 20, transcendentals=0),
        )(scalars, *operands)

    weights = (*halves, *directs[:middle], *directs[middle + 1:])
    own, near, g_all = call(False, (shape((lines,) + packed, F32),), x_own, x_near, c_own, c_near, *weights)
    c_lower = after(c_lower, own)
    c_far = (c_upper, c_lower)
    c_diag = [pp(part, core_swap) for part in c_far]
    far, diagonal, g_own, *g_send = call(
        True, (shape(packed, F32),) + (shape(packed, BF16),) * (lines - 1),
        x_far, x_diag, *c_far, *c_diag, *weights, g_all)

    far = (far.astype(F32) + pp(diagonal, core_swap).astype(F32)).astype(BF16)
    back = pp(far, y_swap)
    received = [pp(g, turn(-r)) for r, g in enumerate(g_send, 1)]
    near = pp(after(near, far), core_swap)
    output, grad_tokens = [(own[n].astype(F32) + near[n].astype(F32) + back[n].astype(F32)).astype(BF16)
                           for n in range(2)]
    grads = []
    for n in range(2):
        total = g_own[n]
        for recv in received:
            total = total + recv[n].astype(F32)
        grads.append(total)
    return output, grad_tokens, grads[0], grads[1]


def solution(mesh):
    in_specs = (
        P(("groups", "tensor"), None),
        P(("groups", "tensor"), None),
        P("tensor", None, None, None),
        P("tensor", None, None, None),
        P(),
        P(),
    )
    out_specs = (
        P(("groups", "tensor"), None),
        P(("groups", "tensor"), None),
        P(("groups", "tensor"), None, None, None),
        P(("groups", "tensor"), None, None, None),
    )
    fn = functools.partial(local, mesh.shape["tensor"], mesh.shape["groups"])
    return jax.shard_map(fn, mesh=mesh, in_specs=in_specs, out_specs=out_specs, check_vma=False)
```
